32 devices in a mesh: row: 16 (over z, y, core), col: 2 (over x).
Axes of the slice: x: 2, y: 2, z: 4, core: 2. Of those that a mesh axis runs over, the one named last changes fastest.
Arguments:
- activation: bfloat16 [1024, 1024, 128], P('row', 'col'), may hold values from -6 to 6
- kernel_one: bfloat16 [3, 3, 128, 128], replicated, may hold values from -0.1875 to 0.1875
- bias_one: float32 [128], replicated, may hold values from -0.5 to 0.5
- kernel_two: bfloat16 [3, 3, 128, 128], replicated, may hold values from -0.1875 to 0.1875
- bias_two: float32 [128], replicated, may hold values from -0.5 to 0.5
Outputs:
- result_map: bfloat16 [1024, 1024, 128], P('row', 'col')
The draws below stay inside these ranges and needn't reach their ends.
All inputs are finite; a program needn't handle non-finite values.
Results may differ from the reference program's by a relative error of at most 0.0095.
Values may be sent and summed in bfloat16 or wider, within the bound.
No kernel may reach another device: no remote copies, remote signals or barrier semaphores. Data moves between devices by JAX's collectives and lax.ppermute only.
A program may use at most 128 MiB of HBM per device.

```python
import jax
import jax.numpy as jnp
from jax import lax

CH = 128
BLOCK = 64
NMAP = 1024
N_ROW = 16


def steps_of(rng, shape, shards, low, largest):
    loudness, own = 1.0, jax.random.fold_in(rng, 6)
    for axis_at, parts in shards:
        heights = jnp.exp(jax.random.uniform(jax.random.fold_in(own, axis_at), (parts,), jnp.float32, low / len(shards), largest / len(shards)))
        loudness = loudness * jnp.repeat(heights, shape[axis_at] // parts).reshape([-1 if axis == axis_at else 1 for axis in range(len(shape))])
    return loudness


def noise(key, extent, spread, limit, cuts=(), kind=jnp.bfloat16):
    array = jax.random.normal(key, extent, jnp.float32) * spread
    if len(cuts) > 0:
        array = steps_of(key, extent, cuts, -0.22, 0.18) * array
    return jnp.clip(array, min=-limit, max=limit).astype(kind)


def setup_inputs(seed: int = 0) -> dict:
    seeds = jax.random.split(jax.random.key(seed), 6)
    activation = noise(seeds[0], (NMAP, NMAP, CH), 1.0, 6.0, ((0, 16), (1, 2)))
    kernel_one = noise(seeds[1], (3, 3, CH, CH), (9 * CH) ** -0.5, 0.1875)
    bias_one = jnp.clip(jax.random.uniform(seeds[2], (CH,), jnp.float32, -0.5, 0.5), -0.5, 0.5)
    kernel_two = noise(seeds[3], (3, 3, CH, CH), (9 * CH) ** -0.5, 0.1875)
    bias_two = jnp.clip(jax.random.uniform(seeds[4], (CH,), jnp.float32, -0.5, 0.5), -0.5, 0.5)
    return {"activation": activation, "kernel_one": kernel_one, "bias_one": bias_one, "kernel_two": kernel_two, "bias_two": bias_two}


def convolve(padded_map, kernel, offset, start):
    band = lax.dynamic_slice_in_dim(padded_map, start, BLOCK + 8, 0).astype(jnp.float32)
    result = lax.conv_general_dilated(band[None], kernel.astype(jnp.float32), (1, 1), "VALID", rhs_dilation=(4, 4), dimension_numbers=("NHWC", "HWIO", "NHWC"), precision=lax.Precision.HIGHEST)[0]
    return result + offset


def reference(activation, kernel_one, bias_one, kernel_two, bias_two):
    padded_in = jnp.pad(activation, ((4, 4), (4, 4), (0, 0)))
    starts = jnp.arange(N_ROW, dtype=jnp.int32) * BLOCK

    def first_layer(start):
        return jax.nn.elu(convolve(padded_in, kernel_one, bias_one, start)).astype(jnp.bfloat16)

    elu_out = lax.map(first_layer, starts).reshape(NMAP, NMAP, CH)
    symmetric = (0.5 * (elu_out.astype(jnp.float32) + jnp.swapaxes(elu_out, 0, 1).astype(jnp.float32))).astype(jnp.bfloat16)
    padded_sym = jnp.pad(symmetric, ((4, 4), (4, 4), (0, 0)))

    def second_layer(start):
        resid = lax.dynamic_slice_in_dim(symmetric, start, BLOCK, 0).astype(jnp.float32)
        return (resid + convolve(padded_sym, kernel_two, bias_two, start)).astype(jnp.bfloat16)

    return lax.map(second_layer, starts).reshape(NMAP, NMAP, CH)
```

```python
import functools

import jax
import jax.numpy as jnp
from jax import lax
from jax.experimental import pallas as pl
from jax.experimental.pallas import tpu as pltpu
from jax.sharding import PartitionSpec as P

REACH = 4
PAIR = 2 * REACH


def conv_kernel(steps, finish, first, odd, even, low, high, left, right, weights, offset, *rest):
    result, taps = rest[-2:]
    extra = rest[:-2]
    step = pl.program_id(0)
    cols = odd.shape[1]

    def widen(group, rows):
        slot = lax.rem(group + 4, 4)
        for r in range(REACH):
            line = rows[r]
            before = left[REACH * (group + 1) + r]
            after = right[REACH * (group + 1) + r]
            taps[slot, r] = jnp.concatenate(
                [
                    jnp.concatenate([before, line[: cols - REACH]], axis=0),
                    line,
                    jnp.concatenate([line[REACH:], after], axis=0),
                ],
                axis=1,
            )

    @pl.when(step == 0)
    def _():
        widen(-1, low)
        widen(0, first)

    widen(2 * step + 1, odd)

    @pl.when(step < steps - 1)
    def _():
        widen(2 * step + 2, even)

    @pl.when(step == steps - 1)
    def _():
        widen(2 * step + 2, high)

    slots = [lax.rem(2 * step + 3 + i, 4) for i in range(4)]
    for r in range(REACH):
        lines = jnp.concatenate([taps[slot, r] for slot in slots], axis=1)
        both = jnp.dot(lines, weights[...], preferred_element_type=jnp.float32)
        half = both.shape[1] // 2
        for i in range(2):
            value = both[:, half * i : half * (i + 1)] + offset[...]
            result[REACH * i + r] = finish(value, extra, REACH * i + r).astype(result.dtype)


def conv(block, low, high, left, right, kernel, offset, finish, extra=()):
    rows, cols, channels = block.shape
    steps = rows // PAIR
    taps = kernel.reshape(3, 3 * channels, channels)
    blank = jnp.zeros((3 * channels, channels), taps.dtype)
    weights = jnp.concatenate(
        [
            jnp.concatenate([taps[0], taps[1], taps[2], blank], axis=0),
            jnp.concatenate([blank, taps[0], taps[1], taps[2]], axis=0),
        ],
        axis=1,
    )
    four = (REACH, cols, channels)
    eight = pl.BlockSpec((PAIR, cols, channels), lambda g: (g, 0, 0))
    whole = pl.BlockSpec(memory_space=pltpu.VMEM)
    flops = 2 * rows * cols * channels * channels * 12
    moved = 2 * (2 + len(extra)) * rows * cols * channels
    return pl.pallas_call(
        functools.partial(conv_kernel, steps, finish),
        grid=(steps,),
        out_shape=jax.ShapeDtypeStruct(block.shape, jnp.bfloat16),
        in_specs=[
            pl.BlockSpec(four, lambda g: (0, 0, 0)),
            pl.BlockSpec(four, lambda g: (2 * g + 1, 0, 0)),
            pl.BlockSpec(four, lambda g: (jnp.minimum(2 * g + 2, 2 * steps - 1), 0, 0)),
            whole,
            whole,
            whole,
            whole,
            whole,
            whole,
        ]
        + [eight] * len(extra),
        out_specs=eight,
        scratch_shapes=[pltpu.VMEM((4, REACH, cols, 3 * channels), jnp.bfloat16)],
        compiler_params=pltpu.CompilerParams(vmem_limit_bytes=48 * 1024 * 1024),
        cost_estimate=pl.CostEstimate(flops=flops, bytes_accessed=moved, transcendentals=0),
    )(block, block, block, low, high, left, right, weights, offset.reshape(1, channels), *extra)


def finish_first(value, extra, r):
    return jnp.where(value > 0, value, jnp.exp(jnp.minimum(value, 0.0)) - 1.0)


def finish_second(value, extra, r):
    return value + extra[0][r].astype(jnp.float32)


def halos(block):
    def step(part, axis, up):
        count = lax.axis_size(axis)
        return lax.ppermute(
            part, axis, [(i, i + 1) if up else (i + 1, i) for i in range(count - 1)]
        )

    rows, cols = block.shape[:2]
    low = step(block[rows - REACH :], "row", True)
    high = step(block[:REACH], "row", False)
    ends = [
        jnp.concatenate([low[:, cut], block[:, cut], high[:, cut]], axis=0)
        for cut in (slice(cols - REACH, None), slice(0, REACH))
    ]
    return low, high, step(ends[0], "col", True), step(ends[1], "col", False)


def mirror_kernel(place, own, other, result):
    turned = jnp.swapaxes(other[...].astype(jnp.float32), 0, 1)
    result[...] = (0.5 * (own[...].astype(jnp.float32) + turned)).astype(result.dtype)


def symmetrize(own, other, place):
    rows, cols, channels = own.shape
    part = pl.BlockSpec((rows, rows, channels), lambda i, place: (0, place[0], 0))
    return pl.pallas_call(
        mirror_kernel,
        grid_spec=pltpu.PrefetchScalarGridSpec(
            num_scalar_prefetch=1,
            grid=(1,),
            in_specs=[part, pl.BlockSpec(other.shape, lambda i, place: (0, 0, 0))],
            out_specs=part,
        ),
        out_shape=jax.ShapeDtypeStruct(own.shape, own.dtype),
        input_output_aliases={1: 0},
        compiler_params=pltpu.CompilerParams(vmem_limit_bytes=48 * 1024 * 1024),
    )(place.reshape(1), own, other)


def exchange(own):
    rows, cols, channels = own.shape
    n_col = lax.axis_size("col")
    count = lax.axis_size("row") // n_col
    me = lax.rem(lax.axis_index("row"), count)

    def device(quarter, local, col):
        return (quarter * count + local % count) * n_col + col

    places = [(a, m, j) for a in range(n_col) for m in range(count) for j in range(n_col)]
    across = [(device(*p), device(p[0], p[1], n_col - 1 - p[2])) for p in places]
    landed = []
    for shift in range(count):
        block = lax.dynamic_slice_in_dim(own, lax.rem(me + shift, count) * rows, rows, 1)
        if shift % 2:
            pairs = [(device(a, m, j), device(j, m + shift, a)) for a, m, j in places]
        else:
            block = lax.ppermute(block, ("row", "col"), across)
            pairs = [
                (device(a, m, n_col - 1 - j), device(j, m + shift, a)) for a, m, j in places
            ]
        landed.append(lax.ppermute(block, ("row", "col"), pairs))
    result = own
    for shift in range(count):
        result = symmetrize(result, landed[shift], lax.rem(me - shift + count, count))
    return result


def body(activation, kernel_one, bias_one, kernel_two, bias_two):
    elu_out = conv(activation, *halos(activation), kernel_one, bias_one, finish_first)
    symmetric = exchange(elu_out)
    return conv(
        symmetric, *halos(symmetric), kernel_two, bias_two, finish_second, (symmetric,)
    )


def solution(mesh):
    in_specs = (P("row", "col", None), P(), P(), P(), P())
    out_specs = P("row", "col", None)
    return jax.shard_map(body, mesh=mesh, in_specs=in_specs, out_specs=out_specs, check_vma=False)
```

```python
import functools

import jax
import jax.numpy as jnp
from jax import lax
from jax.experimental import pallas as pl
from jax.experimental.pallas import tpu as pltpu
from jax.sharding import PartitionSpec as P

REACH = 4
PAIR = 2 * REACH
ROOM = pltpu.CompilerParams(vmem_limit_bytes=48 * 1024 * 1024)


def widen(taps, slot, rows, before, after):
    cols = rows.shape[1]
    for r in range(REACH):
        line = rows[r]
        taps[slot, r] = jnp.concatenate(
            [
                jnp.concatenate([before[r], line[: cols - REACH]], axis=0),
                line,
                jnp.concatenate([line[REACH:], after[r]], axis=0),
            ],
            axis=1,
        )


def multiply(taps, slots, weights, offset, finish):
    for r in range(REACH):
        lines = jnp.concatenate([taps[slot, r] for slot in slots], axis=1)
        both = jnp.dot(lines, weights[...], preferred_element_type=jnp.float32)
        half = both.shape[1] // 2
        for i in range(2):
            finish(both[:, half * i : half * (i + 1)] + offset[...], REACH * i + r)


def inner_kernel(finish, me, one, two, odd, even, left, right, weights, offset, *rest):
    taps = rest[-1]
    step = pl.program_id(0) + 1

    def fill(group, rows):
        at = pl.ds(REACH * group, REACH)
        widen(taps, lax.rem(group, 4), rows, left[at], right[at])

    @pl.when(step == 1)
    def _():
        fill(1, one)
        fill(2, two)

    fill(2 * step + 1, odd)
    fill(2 * step + 2, even)
    slots = [lax.rem(2 * step + 3 + i, 4) for i in range(4)]
    multiply(taps, slots, weights, offset, functools.partial(finish, me, rest))


def outer_kernel(finish, me, low, high, one, two, three, left, right, weights, offset, *rest):
    taps = rest[-1]
    end = pl.program_id(0)
    cols = one.shape[1]

    def fill(slot, rows):
        at = pl.ds(REACH * slot, REACH)
        widen(taps, slot, rows, left[0, at], right[0, at])

    @pl.when(end == 0)
    def _():
        fill(0, low[:, :cols])

    @pl.when(end == 1)
    def _():
        fill(3, high[:, :cols])

    for i, rows in enumerate((one, two, three)):
        fill(i + 1 - end, rows)
    multiply(taps, range(4), weights, offset, functools.partial(finish, me, rest))


def paired(kernel):
    channels = kernel.shape[-1]
    taps = kernel.reshape(3, 3 * channels, channels)
    blank = jnp.zeros((1, 3 * channels, channels), taps.dtype)
    halves = [jnp.concatenate([taps, blank]), jnp.concatenate([blank, taps])]
    return jnp.concatenate([h.reshape(12 * channels, channels) for h in halves], axis=1)


def conv(block, halos, kernel, offset, finish, shapes, me, extra=(), scratch=()):
    rows, cols, channels = block.shape
    steps, groups = rows // PAIR, rows // REACH
    weights, offset = paired(kernel), offset.reshape(1, channels)
    (left, right), (low, high, left_ends, right_ends) = halos
    four = (REACH, cols, channels)
    whole = pl.BlockSpec(memory_space=pltpu.VMEM)
    scratch = [*scratch, pltpu.VMEM((4, REACH, cols, 3 * channels), jnp.bfloat16)]
    outs = [jax.ShapeDtypeStruct(s, jnp.bfloat16) for s in shapes]

    def slab(shape, step_of):
        size = (*shape[:-3], PAIR, *shape[-2:])
        lead = (0,) * (len(shape) - 3)
        return pl.BlockSpec(size, lambda g, me: (*lead, step_of(g), 0, 0))

    def cost(count):
        work = count * PAIR * cols * channels
        return pl.CostEstimate(
            flops=24 * work * channels, bytes_accessed=8 * work, transcendentals=0
        )

    inner = lambda g: g + 1
    results = pl.pallas_call(
        functools.partial(inner_kernel, finish),
        grid_spec=pltpu.PrefetchScalarGridSpec(
            num_scalar_prefetch=1,
            grid=(steps - 2,),
            in_specs=[
                pl.BlockSpec(four, lambda g, me: (1, 0, 0)),
                pl.BlockSpec(four, lambda g, me: (2, 0, 0)),
                pl.BlockSpec(four, lambda g, me: (2 * g + 3, 0, 0)),
                pl.BlockSpec(four, lambda g, me: (2 * g + 4, 0, 0)),
            ]
            + [whole] * 4
            + [slab(e.shape, inner) for e in extra],
            out_specs=[slab(s, inner) for s in shapes],
            scratch_shapes=scratch,
        ),
        out_shape=outs,
        compiler_params=ROOM,
        cost_estimate=cost(steps - 2),
    )(me, block, block, block, block, left, right, weights, offset, *extra)

    def third(i):
        return pl.BlockSpec(four, lambda e, me: (i + e * (groups - 3), 0, 0))

    def at_end(array):
        return pl.BlockSpec((1, *array.shape[1:]), lambda e, me: (e, 0, 0, 0))

    outer = lambda e: e * (steps - 1)
    given = [me, low, high, block, block, block, left_ends, right_ends, weights, offset, *extra]
    return pl.pallas_call(
        functools.partial(outer_kernel, finish),
        grid_spec=pltpu.PrefetchScalarGridSpec(
            num_scalar_prefetch=1,
            grid=(2,),
            in_specs=[whole, whole, third(0), third(1), third(2)]
            + [at_end(left_ends), at_end(right_ends), whole, whole]
            + [slab(e.shape, outer) for e in extra]
            + [pl.BlockSpec(memory_space=pl.ANY)] * len(outs),
            out_specs=[slab(s, outer) for s in shapes],
            scratch_shapes=scratch,
        ),
        out_shape=outs,
        input_output_aliases={len(given) + i: i for i in range(len(outs))},
        compiler_params=ROOM,
        cost_estimate=cost(2),
    )(*given, *results)


def finish_first(count, groups, me, rest, value, r):
    line, outs = rest[-2], rest[-2 - len(groups) : -2]
    value = jnp.where(value > 0, value, jnp.exp(jnp.minimum(value, 0.0)) - 1.0)
    line[...] = value
    size = outs[0].shape[-2]
    for out, group in zip(outs, groups):
        for n, shift in enumerate(group):
            start = pl.multiple_of(lax.rem(me[0] + shift, count) * size, size)
            out[n, r] = line[pl.ds(start, size)].astype(out.dtype)


def finish_second(me, rest, value, r):
    own, result = rest[0], rest[-2]
    result[r] = (value + own[r].astype(jnp.float32)).astype(result.dtype)


def halos(block):
    def move(part, axis, up):
        count = lax.axis_size(axis)
        return lax.ppermute(
            part, axis, [(i, i + 1) if up else (i + 1, i) for i in range(count - 1)]
        )

    rows, cols = block.shape[:2]
    if lax.axis_size("col") == 2:
        first = lax.axis_index("col") == 0
        edge = jnp.where(first, block[:, cols - REACH :], block[:, :REACH])
        edge = lax.ppermute(edge, "col", [(0, 1), (1, 0)])
        left, right = jnp.where(first, 0, edge), jnp.where(first, edge, 0)
    else:
        left = move(block[:, cols - REACH :], "col", True)
        right = move(block[:, :REACH], "col", False)
    wide = [
        jnp.concatenate([array[cut] for array in (block, left, right)], axis=1)
        for cut in (slice(rows - REACH, None), slice(0, REACH))
    ]
    low, high = move(wide[0], "row", True), move(wide[1], "row", False)
    reach = 3 * REACH
    ends = [
        jnp.stack(
            [
                jnp.concatenate([low[:, at : at + REACH], side[:reach]]),
                jnp.concatenate([side[rows - reach :], high[:, at : at + REACH]]),
            ]
        )
        for at, side in ((cols, left), (cols + REACH, right))
    ]
    return (left, right), (low, high, *ends)


def mirror_kernel(sizes, place, own, *rest):
    result = rest[-1]
    parts = iter(rest)
    start = 0
    for size, choice in sizes:
        other = next(parts)[...].astype(jnp.float32)
        if choice:
            mine = next(parts)[...].astype(jnp.float32)
            other = jnp.where(place[1] == 1, mine, other)
        cut = slice(start, start + size)
        turned = jnp.swapaxes(other, 0, 1)
        value = 0.5 * (own[0, :, cut].astype(jnp.float32) + turned)
        result[:, cut] = value.astype(result.dtype)
        start += size


def symmetrize(so_far, shape, own, index, parts, place):
    rows, channels = own.shape[1], own.shape[3]
    arrays = [array for part in parts for array in part]
    sizes = [(part[0].shape[0], len(part) > 1) for part in parts]
    out = pl.BlockSpec((rows, rows, channels), lambda i, place: (0, place[0], 0))
    given = [place, own, *arrays]
    first = so_far is None
    return pl.pallas_call(
        functools.partial(mirror_kernel, sizes),
        grid_spec=pltpu.PrefetchScalarGridSpec(
            num_scalar_prefetch=1,
            grid=(1,),
            in_specs=[pl.BlockSpec((1, rows, rows, channels), lambda i, place: (index, 0, 0, 0))]
            + [pl.BlockSpec(a.shape, lambda i, place: (0, 0, 0)) for a in arrays]
            + [pl.BlockSpec(memory_space=pl.ANY)] * (not first),
            out_specs=out,
        ),
        out_shape=jax.ShapeDtypeStruct(shape, own.dtype),
        input_output_aliases={} if first else {len(given): 0},
        compiler_params=ROOM,
    )(*given, *([] if first else [so_far]))


def groups_of(n_col, count):
    if n_col != 2 or count < 4:
        return [(s,) for s in range(count)]
    return [(s,) for s in range(count)]


def exchange(pieces, shape, me):
    n_col = lax.axis_size("col")
    count = lax.axis_size("row") // n_col
    rows, channels = shape[0], shape[2]
    mine = (lax.axis_index("row") // count == lax.axis_index("col")).astype(jnp.int32)
    groups = groups_of(n_col, count)
    where = {s: (i, n) for i, group in enumerate(groups) for n, s in enumerate(group)}

    def device(quarter, local, col):
        return (quarter * count + local % count) * n_col + col

    places = [(a, m, j) for a in range(n_col) for m in range(count) for j in range(n_col)]

    def send(block, pairs):
        return lax.ppermute(block, ("row", "col"), pairs)

    def direct(block, shift):
        return send(block, [(device(*p), device(p[2], p[1] + shift, p[0])) for p in places])

    def piece(shift):
        i, n = where[shift]
        return pieces[i][n]

    landed = {}
    if n_col != 2:
        for s in range(count):
            landed[s] = [(direct(piece(s), s),)]
    else:
        across = [(device(*p), device(p[0], p[1], 1 - p[2])) for p in places]
        for s in range(count):
            if s % 2:
                landed[s] = [(direct(piece(s), s),)]
            else:
                hop = send(piece(s), across)
                pairs = [(device(a, m, 1 - j), device(j, m + s, a)) for a, m, j in places]
                landed[s] = [(send(hop, pairs),)]
    result = None
    for s in [s for s in range(count) if s in landed] + [s for s in landed if s > 7]:
        i, n = where[-s % count]
        place = jnp.stack([lax.rem(me[0] - s + count, count), mine])
        result = symmetrize(result, shape, pieces[i], n, landed[s], place)
    return result


def body(activation, kernel_one, bias_one, kernel_two, bias_two):
    rows, cols, channels = activation.shape
    n_col = lax.axis_size("col")
    count = lax.axis_size("row") // n_col
    me = lax.rem(lax.axis_index("row"), count).astype(jnp.int32).reshape(1)
    groups = groups_of(n_col, count)
    shapes = [(len(g), rows, rows, channels) for g in groups]
    pieces = conv(
        activation,
        halos(activation),
        kernel_one,
        bias_one,
        functools.partial(finish_first, count, groups),
        shapes,
        me,
        scratch=(pltpu.VMEM((cols, channels), jnp.float32),),
    )
    symmetric = exchange(pieces, activation.shape, me)
    return conv(
        symmetric,
        halos(symmetric),
        kernel_two,
        bias_two,
        finish_second,
        [activation.shape],
        me,
        extra=(symmetric,),
    )[0]


def solution(mesh):
    in_specs = (P("row", "col", None), P(), P(), P(), P())
    out_specs = P("row", "col", None)
    return jax.shard_map(body, mesh=mesh, in_specs=in_specs, out_specs=out_specs, check_vma=False)
```

```python
import functools

import jax
import jax.numpy as jnp
from jax import lax
from jax.experimental import pallas as pl
from jax.experimental.pallas import tpu as pltpu
from jax.sharding import PartitionSpec as P

REACH = 4
PAIR = 2 * REACH
ROOM = pltpu.CompilerParams(vmem_limit_bytes=48 * 1024 * 1024)


def widen(taps, slot, rows, before, after):
    cols = rows.shape[1]
    for r in range(REACH):
        line = rows[r]
        taps[slot, r] = jnp.concatenate(
            [
                jnp.concatenate([before[r], line[: cols - REACH]], axis=0),
                line,
                jnp.concatenate([line[REACH:], after[r]], axis=0),
            ],
            axis=1,
        )


def multiply(taps, slots, weights, offset, finish):
    for r in range(REACH):
        lines = jnp.concatenate([taps[slot, r] for slot in slots], axis=1)
        both = jnp.dot(lines, weights[...], preferred_element_type=jnp.float32)
        half = both.shape[1] // 2
        for i in range(2):
            finish(both[:, half * i : half * (i + 1)] + offset[...], REACH * i + r)


def inner_kernel(finish, me, one, two, odd, even, left, right, weights, offset, *rest):
    taps = rest[-1]
    step = pl.program_id(0) + 1

    def fill(group, rows):
        at = pl.ds(REACH * group, REACH)
        widen(taps, lax.rem(group, 4), rows, left[at], right[at])

    @pl.when(step == 1)
    def _():
        fill(1, one)
        fill(2, two)

    fill(2 * step + 1, odd)
    fill(2 * step + 2, even)
    slots = [lax.rem(2 * step + 3 + i, 4) for i in range(4)]
    multiply(taps, slots, weights, offset, functools.partial(finish, me, rest))


def outer_kernel(finish, me, low, high, one, two, three, left, right, weights, offset, *rest):
    taps = rest[-1]
    end = pl.program_id(0)
    cols = one.shape[1]

    def fill(slot, rows):
        at = pl.ds(REACH * slot, REACH)
        widen(taps, slot, rows, left[0, at], right[0, at])

    @pl.when(end == 0)
    def _():
        fill(0, low[:, :cols])

    @pl.when(end == 1)
    def _():
        fill(3, high[:, :cols])

    for i, rows in enumerate((one, two, three)):
        fill(i + 1 - end, rows)
    multiply(taps, range(4), weights, offset, functools.partial(finish, me, rest))


def paired(kernel):
    channels = kernel.shape[-1]
    taps = kernel.reshape(3, 3 * channels, channels)
    blank = jnp.zeros((1, 3 * channels, channels), taps.dtype)
    halves = [jnp.concatenate([taps, blank]), jnp.concatenate([blank, taps])]
    return jnp.concatenate([h.reshape(12 * channels, channels) for h in halves], axis=1)


def conv(block, halos, kernel, offset, finish, shapes, me, extra=(), scratch=()):
    rows, cols, channels = block.shape
    steps, groups = rows // PAIR, rows // REACH
    weights, offset = paired(kernel), offset.reshape(1, channels)
    (left, right), (low, high, left_ends, right_ends) = halos
    four = (REACH, cols, channels)
    whole = pl.BlockSpec(memory_space=pltpu.VMEM)
    scratch = [*scratch, pltpu.VMEM((4, REACH, cols, 3 * channels), jnp.bfloat16)]
    outs = [jax.ShapeDtypeStruct(s, jnp.bfloat16) for s in shapes]

    def slab(shape, step_of):
        size = (*shape[:-3], PAIR, *shape[-2:])
        lead = (0,) * (len(shape) - 3)
        return pl.BlockSpec(size, lambda g, me: (*lead, step_of(g), 0, 0))

    def cost(count):
        work = count * PAIR * cols * channels
        return pl.CostEstimate(
            flops=24 * work * channels, bytes_accessed=8 * work, transcendentals=0
        )

    inner = lambda g: g + 1
    results = pl.pallas_call(
        functools.partial(inner_kernel, finish),
        grid_spec=pltpu.PrefetchScalarGridSpec(
            num_scalar_prefetch=1,
            grid=(steps - 2,),
            in_specs=[
                pl.BlockSpec(four, lambda g, me: (1, 0, 0)),
                pl.BlockSpec(four, lambda g, me: (2, 0, 0)),
                pl.BlockSpec(four, lambda g, me: (2 * g + 3, 0, 0)),
                pl.BlockSpec(four, lambda g, me: (2 * g + 4, 0, 0)),
            ]
            + [whole] * 4
            + [slab(e.shape, inner) for e in extra],
            out_specs=[slab(s, inner) for s in shapes],
            scratch_shapes=scratch,
        ),
        out_shape=outs,
        compiler_params=ROOM,
        cost_estimate=cost(steps - 2),
    )(me, block, block, block, block, left, right, weights, offset, *extra)

    def third(i):
        return pl.BlockSpec(four, lambda e, me: (i + e * (groups - 3), 0, 0))

    def at_end(array):
        return pl.BlockSpec((1, *array.shape[1:]), lambda e, me: (e, 0, 0, 0))

    outer = lambda e: e * (steps - 1)
    given = [me, low, high, block, block, block, left_ends, right_ends, weights, offset, *extra]
    return pl.pallas_call(
        functools.partial(outer_kernel, finish),
        grid_spec=pltpu.PrefetchScalarGridSpec(
            num_scalar_prefetch=1,
            grid=(2,),
            in_specs=[whole, whole, third(0), third(1), third(2)]
            + [at_end(left_ends), at_end(right_ends), whole, whole]
            + [slab(e.shape, outer) for e in extra]
            + [pl.BlockSpec(memory_space=pl.ANY)] * len(outs),
            out_specs=[slab(s, outer) for s in shapes],
            scratch_shapes=scratch,
        ),
        out_shape=outs,
        input_output_aliases={len(given) + i: i for i in range(len(outs))},
        compiler_params=ROOM,
        cost_estimate=cost(2),
    )(*given, *results)


def finish_first(count, groups, me, rest, value, r):
    line, outs = rest[-2], rest[-2 - len(groups) : -2]
    value = jnp.where(value > 0, value, jnp.exp(jnp.minimum(value, 0.0)) - 1.0)
    line[...] = value
    size = outs[0].shape[-2]
    for out, group in zip(outs, groups):
        for n, shift in enumerate(group):
            start = pl.multiple_of(lax.rem(me[0] + shift, count) * size, size)
            out[n, r] = line[pl.ds(start, size)].astype(out.dtype)


def finish_second(me, rest, value, r):
    own, result = rest[0], rest[-2]
    result[r] = (value + own[r].astype(jnp.float32)).astype(result.dtype)


def halos(block):
    def move(part, axis, up):
        count = lax.axis_size(axis)
        return lax.ppermute(
            part, axis, [(i, i + 1) if up else (i + 1, i) for i in range(count - 1)]
        )

    rows, cols = block.shape[:2]
    if lax.axis_size("col") == 2:
        first = lax.axis_index("col") == 0
        edge = jnp.where(first, block[:, cols - REACH :], block[:, :REACH])
        edge = lax.ppermute(edge, "col", [(0, 1), (1, 0)])
        left, right = jnp.where(first, 0, edge), jnp.where(first, edge, 0)
    else:
        left = move(block[:, cols - REACH :], "col", True)
        right = move(block[:, :REACH], "col", False)
    wide = [
        jnp.concatenate([array[cut] for array in (block, left, right)], axis=1)
        for cut in (slice(rows - REACH, None), slice(0, REACH))
    ]
    low, high = move(wide[0], "row", True), move(wide[1], "row", False)
    reach = 3 * REACH
    ends = [
        jnp.stack(
            [
                jnp.concatenate([low[:, at : at + REACH], side[:reach]]),
                jnp.concatenate([side[rows - reach :], high[:, at : at + REACH]]),
            ]
        )
        for at, side in ((cols, left), (cols + REACH, right))
    ]
    return (left, right), (low, high, *ends)


def mirror_kernel(sizes, place, own, *rest):
    result = rest[-1]
    parts = iter(rest)
    start = 0
    for size, choice in sizes:
        other = next(parts)[...].astype(jnp.float32)
        if choice:
            mine = next(parts)[...].astype(jnp.float32)
            other = jnp.where(place[1] == 1, mine, other)
        cut = slice(start, start + size)
        turned = jnp.swapaxes(other, 0, 1)
        value = 0.5 * (own[0, :, cut].astype(jnp.float32) + turned)
        result[:, cut] = value.astype(result.dtype)
        start += size


def symmetrize(so_far, shape, own, index, parts, place):
    rows, channels = own.shape[1], own.shape[3]
    arrays = [array for part in parts for array in part]
    sizes = [(part[0].shape[0], len(part) > 1) for part in parts]
    out = pl.BlockSpec((rows, rows, channels), lambda i, place: (0, place[0], 0))
    given = [place, own, *arrays]
    first = so_far is None
    return pl.pallas_call(
        functools.partial(mirror_kernel, sizes),
        grid_spec=pltpu.PrefetchScalarGridSpec(
            num_scalar_prefetch=1,
            grid=(1,),
            in_specs=[pl.BlockSpec((1, rows, rows, channels), lambda i, place: (index, 0, 0, 0))]
            + [pl.BlockSpec(a.shape, lambda i, place: (0, 0, 0)) for a in arrays]
            + [pl.BlockSpec(memory_space=pl.ANY)] * (not first),
            out_specs=out,
        ),
        out_shape=jax.ShapeDtypeStruct(shape, own.dtype),
        input_output_aliases={} if first else {len(given): 0},
        compiler_params=ROOM,
    )(*given, *([] if first else [so_far]))


def groups_of(n_col, count):
    if n_col != 2 or count < 4:
        return [(s,) for s in range(count)]
    return [(s,) for s in range(count)]


def exchange(pieces, shape, me):
    n_col = lax.axis_size("col")
    count = lax.axis_size("row") // n_col
    rows, channels = shape[0], shape[2]
    mine = (lax.axis_index("row") // count == lax.axis_index("col")).astype(jnp.int32)
    groups = groups_of(n_col, count)
    where = {s: (i, n) for i, group in enumerate(groups) for n, s in enumerate(group)}

    def device(quarter, local, col):
        return (quarter * count + local % count) * n_col + col

    places = [(a, m, j) for a in range(n_col) for m in range(count) for j in range(n_col)]

    def send(block, pairs):
        return lax.ppermute(block, ("row", "col"), pairs)

    def direct(block, shift):
        return send(block, [(device(*p), device(p[2], p[1] + shift, p[0])) for p in places])

    def piece(shift):
        i, n = where[shift]
        return pieces[i][n]

    landed = {}
    if n_col != 2:
        for s in range(count):
            landed[s] = [(direct(piece(s), s),)]
    else:
        across = [(device(*p), device(p[0], p[1], 1 - p[2])) for p in places]
        for s in range(count):
            if s % 2:
                landed[s] = [(direct(piece(s), s),)]
            else:
                hop = send(piece(s), across)
                pairs = [(device(a, m, 1 - j), device(j, m + s, a)) for a, m, j in places]
                landed[s] = [(send(hop, pairs),)]
    result = None
    for s in sorted(landed, key=lambda s: s ^ 1):
        i, n = where[-s % count]
        place = jnp.stack([lax.rem(me[0] - s + count, count), mine])
        result = symmetrize(result, shape, pieces[i], n, landed[s], place)
    return result


def body(activation, kernel_one, bias_one, kernel_two, bias_two):
    rows, cols, channels = activation.shape
    n_col = lax.axis_size("col")
    count = lax.axis_size("row") // n_col
    me = lax.rem(lax.axis_index("row"), count).astype(jnp.int32).reshape(1)
    groups = groups_of(n_col, count)
    shapes = [(len(g), rows, rows, channels) for g in groups]
    pieces = conv(
        activation,
        halos(activation),
        kernel_one,
        bias_one,
        functools.partial(finish_first, count, groups),
        shapes,
        me,
        scratch=(pltpu.VMEM((cols, channels), jnp.float32),),
    )
    symmetric = exchange(pieces, activation.shape, me)
    return conv(
        symmetric,
        halos(symmetric),
        kernel_two,
        bias_two,
        finish_second,
        [activation.shape],
        me,
        extra=(symmetric,),
    )[0]


def solution(mesh):
    in_specs = (P("row", "col", None), P(), P(), P(), P())
    out_specs = P("row", "col", None)
    return jax.shard_map(body, mesh=mesh, in_specs=in_specs, out_specs=out_specs, check_vma=False)
```

```python
import functools

import jax
import jax.numpy as jnp
from jax import lax
from jax.experimental import pallas as pl
from jax.experimental.pallas import tpu as pltpu
from jax.sharding import PartitionSpec as P

REACH = 4
PAIR = 2 * REACH
ROOM = pltpu.CompilerParams(vmem_limit_bytes=48 * 1024 * 1024)


def widen(taps, slot, rows, before, after):
    cols = rows.shape[1]
    for r in range(REACH):
        line = rows[r]
        taps[slot, r] = jnp.concatenate(
            [
                jnp.concatenate([before[r], line[: cols - REACH]], axis=0),
                line,
                jnp.concatenate([line[REACH:], after[r]], axis=0),
            ],
            axis=1,
        )


def multiply(taps, slots, weights, offset, finish):
    for r in range(REACH):
        lines = jnp.concatenate([taps[slot, r] for slot in slots], axis=1)
        both = jnp.dot(lines, weights[...], preferred_element_type=jnp.float32)
        half = both.shape[1] // 2
        for i in range(2):
            finish(both[:, half * i : half * (i + 1)] + offset[...], REACH * i + r)


def inner_kernel(finish, me, one, two, odd, even, left, right, weights, offset, *rest):
    taps = rest[-1]
    step = pl.program_id(0) + 1

    def fill(group, rows):
        at = pl.ds(REACH * group, REACH)
        widen(taps, lax.rem(group, 4), rows, left[at], right[at])

    @pl.when(step == 1)
    def _():
        fill(1, one)
        fill(2, two)

    fill(2 * step + 1, odd)
    fill(2 * step + 2, even)
    slots = [lax.rem(2 * step + 3 + i, 4) for i in range(4)]
    multiply(taps, slots, weights, offset, functools.partial(finish, me, rest))


def outer_kernel(finish, me, low, high, one, two, three, left, right, weights, offset, *rest):
    taps = rest[-1]
    end = pl.program_id(0)
    cols = one.shape[1]

    def fill(slot, rows):
        at = pl.ds(REACH * slot, REACH)
        widen(taps, slot, rows, left[0, at], right[0, at])

    @pl.when(end == 0)
    def _():
        fill(0, low[:, :cols])

    @pl.when(end == 1)
    def _():
        fill(3, high[:, :cols])

    for i, rows in enumerate((one, two, three)):
        fill(i + 1 - end, rows)
    multiply(taps, range(4), weights, offset, functools.partial(finish, me, rest))


def paired(kernel):
    channels = kernel.shape[-1]
    taps = kernel.reshape(3, 3 * channels, channels)
    blank = jnp.zeros((1, 3 * channels, channels), taps.dtype)
    halves = [jnp.concatenate([taps, blank]), jnp.concatenate([blank, taps])]
    return jnp.concatenate([h.reshape(12 * channels, channels) for h in halves], axis=1)


def conv(block, halos, kernel, offset, finish, shapes, me, extra=(), scratch=()):
    rows, cols, channels = block.shape
    steps, groups = rows // PAIR, rows // REACH
    weights, offset = paired(kernel), offset.reshape(1, channels)
    (left, right), (low, high, left_ends, right_ends) = halos
    four = (REACH, cols, channels)
    whole = pl.BlockSpec(memory_space=pltpu.VMEM)
    scratch = [*scratch, pltpu.VMEM((4, REACH, cols, 3 * channels), jnp.bfloat16)]
    outs = [jax.ShapeDtypeStruct(s, jnp.bfloat16) for s in shapes]

    def slab(shape, step_of):
        size = (*shape[:-3], PAIR, *shape[-2:])
        lead = (0,) * (len(shape) - 3)
        return pl.BlockSpec(size, lambda g, me: (*lead, step_of(g), 0, 0))

    def cost(count):
        work = count * PAIR * cols * channels
        return pl.CostEstimate(
            flops=24 * work * channels, bytes_accessed=8 * work, transcendentals=0
        )

    inner = lambda g: g + 1
    results = pl.pallas_call(
        functools.partial(inner_kernel, finish),
        grid_spec=pltpu.PrefetchScalarGridSpec(
            num_scalar_prefetch=1,
            grid=(steps - 2,),
            in_specs=[
                pl.BlockSpec(four, lambda g, me: (1, 0, 0)),
                pl.BlockSpec(four, lambda g, me: (2, 0, 0)),
                pl.BlockSpec(four, lambda g, me: (2 * g + 3, 0, 0)),
                pl.BlockSpec(four, lambda g, me: (2 * g + 4, 0, 0)),
            ]
            + [whole] * 4
            + [slab(e.shape, inner) for e in extra],
            out_specs=[slab(s, inner) for s in shapes],
            scratch_shapes=scratch,
        ),
        out_shape=outs,
        compiler_params=ROOM,
        cost_estimate=cost(steps - 2),
    )(me, block, block, block, block, left, right, weights, offset, *extra)

    def third(i):
        return pl.BlockSpec(four, lambda e, me: (i + e * (groups - 3), 0, 0))

    def at_end(array):
        return pl.BlockSpec((1, *array.shape[1:]), lambda e, me: (e, 0, 0, 0))

    outer = lambda e: e * (steps - 1)
    given = [me, low, high, block, block, block, left_ends, right_ends, weights, offset, *extra]
    return pl.pallas_call(
        functools.partial(outer_kernel, finish),
        grid_spec=pltpu.PrefetchScalarGridSpec(
            num_scalar_prefetch=1,
            grid=(2,),
            in_specs=[whole, whole, third(0), third(1), third(2)]
            + [at_end(left_ends), at_end(right_ends), whole, whole]
            + [slab(e.shape, outer) for e in extra]
            + [pl.BlockSpec(memory_space=pl.ANY)] * len(outs),
            out_specs=[slab(s, outer) for s in shapes],
            scratch_shapes=scratch,
        ),
        out_shape=outs,
        input_output_aliases={len(given) + i: i for i in range(len(outs))},
        compiler_params=ROOM,
        cost_estimate=cost(2),
    )(*given, *results)


def finish_first(count, groups, me, rest, value, r):
    line, outs = rest[-2], rest[-2 - len(groups) : -2]
    value = jnp.where(value > 0, value, jnp.exp(jnp.minimum(value, 0.0)) - 1.0)
    line[...] = value
    size = outs[0].shape[-2]
    for out, group in zip(outs, groups):
        for n, shift in enumerate(group):
            start = pl.multiple_of(lax.rem(me[0] + shift, count) * size, size)
            out[n, r] = line[pl.ds(start, size)].astype(out.dtype)


def finish_second(me, rest, value, r):
    own, result = rest[0], rest[-2]
    result[r] = (value + own[r].astype(jnp.float32)).astype(result.dtype)


def halos(block):
    def move(part, axis, up):
        count = lax.axis_size(axis)
        return lax.ppermute(
            part, axis, [(i, i + 1) if up else (i + 1, i) for i in range(count - 1)]
        )

    rows, cols = block.shape[:2]
    if lax.axis_size("col") == 2:
        first = lax.axis_index("col") == 0
        edge = jnp.where(first, block[:, cols - REACH :], block[:, :REACH])
        edge = lax.ppermute(edge, "col", [(0, 1), (1, 0)])
        left, right = jnp.where(first, 0, edge), jnp.where(first, edge, 0)
    else:
        left = move(block[:, cols - REACH :], "col", True)
        right = move(block[:, :REACH], "col", False)
    wide = [
        jnp.concatenate([array[cut] for array in (block, left, right)], axis=1)
        for cut in (slice(rows - REACH, None), slice(0, REACH))
    ]
    low, high = move(wide[0], "row", True), move(wide[1], "row", False)
    reach = 3 * REACH
    ends = [
        jnp.stack(
            [
                jnp.concatenate([low[:, at : at + REACH], side[:reach]]),
                jnp.concatenate([side[rows - reach :], high[:, at : at + REACH]]),
            ]
        )
        for at, side in ((cols, left), (cols + REACH, right))
    ]
    return (left, right), (low, high, *ends)


def mirror_kernel(sizes, place, own, *rest):
    result = rest[-1]
    parts = iter(rest)
    start = 0
    for size, choice in sizes:
        other = next(parts)[...].astype(jnp.float32)
        if choice:
            mine = next(parts)[...].astype(jnp.float32)
            other = jnp.where(place[1] == 1, mine, other)
        cut = slice(start, start + size)
        turned = jnp.swapaxes(other, 0, 1)
        value = 0.5 * (own[0, :, cut].astype(jnp.float32) + turned)
        result[:, cut] = value.astype(result.dtype)
        start += size


def symmetrize(so_far, shape, own, index, parts, place):
    rows, channels = own.shape[1], own.shape[3]
    arrays = [array for part in parts for array in part]
    sizes = [(part[0].shape[0], len(part) > 1) for part in parts]
    out = pl.BlockSpec((rows, rows, channels), lambda i, place: (0, place[0], 0))
    given = [place, own, *arrays]
    first = so_far is None
    return pl.pallas_call(
        functools.partial(mirror_kernel, sizes),
        grid_spec=pltpu.PrefetchScalarGridSpec(
            num_scalar_prefetch=1,
            grid=(1,),
            in_specs=[pl.BlockSpec((1, rows, rows, channels), lambda i, place: (index, 0, 0, 0))]
            + [pl.BlockSpec(a.shape, lambda i, place: (0, 0, 0)) for a in arrays]
            + [pl.BlockSpec(memory_space=pl.ANY)] * (not first),
            out_specs=out,
        ),
        out_shape=jax.ShapeDtypeStruct(shape, own.dtype),
        input_output_aliases={} if first else {len(given): 0},
        compiler_params=ROOM,
    )(*given, *([] if first else [so_far]))


def groups_of(n_col, count):
    if n_col != 2 or count < 4:
        return [(s,) for s in range(count)]
    return [(s,) for s in range(count)]


def exchange(pieces, shape, me):
    n_col = lax.axis_size("col")
    count = lax.axis_size("row") // n_col
    rows, channels = shape[0], shape[2]
    mine = (lax.axis_index("row") // count == lax.axis_index("col")).astype(jnp.int32)
    groups = groups_of(n_col, count)
    where = {s: (i, n) for i, group in enumerate(groups) for n, s in enumerate(group)}

    def device(quarter, local, col):
        return (quarter * count + local % count) * n_col + col

    places = [(a, m, j) for a in range(n_col) for m in range(count) for j in range(n_col)]

    def send(block, pairs):
        return lax.ppermute(block, ("row", "col"), pairs)

    def direct(block, shift):
        return send(block, [(device(*p), device(p[2], p[1] + shift, p[0])) for p in places])

    def piece(shift):
        i, n = where[shift]
        return pieces[i][n]

    landed = {}
    if n_col != 2:
        for s in range(count):
            landed[s] = [(direct(piece(s), s),)]
    else:
        for s in range(count):
            if s % 2:
                landed[s] = [(direct(piece(s), s),)]
            else:
                away = [p for p in places if s or p[0] != p[2]]
                hop = send(piece(s), [(device(*p), device(p[0], p[1], 1 - p[2])) for p in away])
                pairs = [(device(a, m, 1 - j), device(j, m + s, a)) for a, m, j in away]
                landed[s] = [(send(hop, pairs),) if s else (send(hop, pairs), piece(0))]
    result = None
    for s in [s for s in range(count) if s in landed] + [s for s in landed if s > 7]:
        i, n = where[-s % count]
        place = jnp.stack([lax.rem(me[0] - s + count, count), mine])
        result = symmetrize(result, shape, pieces[i], n, landed[s], place)
    return result


def body(activation, kernel_one, bias_one, kernel_two, bias_two):
    rows, cols, channels = activation.shape
    n_col = lax.axis_size("col")
    count = lax.axis_size("row") // n_col
    me = lax.rem(lax.axis_index("row"), count).astype(jnp.int32).reshape(1)
    groups = groups_of(n_col, count)
    shapes = [(len(g), rows, rows, channels) for g in groups]
    pieces = conv(
        activation,
        halos(activation),
        kernel_one,
        bias_one,
        functools.partial(finish_first, count, groups),
        shapes,
        me,
        scratch=(pltpu.VMEM((cols, channels), jnp.float32),),
    )
    symmetric = exchange(pieces, activation.shape, me)
    return conv(
        symmetric,
        halos(symmetric),
        kernel_two,
        bias_two,
        finish_second,
        [activation.shape],
        me,
        extra=(symmetric,),
    )[0]


def solution(mesh):
    in_specs = (P("row", "col", None), P(), P(), P(), P())
    out_specs = P("row", "col", None)
    return jax.shard_map(body, mesh=mesh, in_specs=in_specs, out_specs=out_specs, check_vma=False)
```
